32 devices in a mesh: tiles: 2 (over y), acq: 8 (over z, x), pix: 2 (over core).
Axes of the slice: x: 2, y: 2, z: 4, core: 2. Of those that a mesh axis runs over, the one named last changes fastest.
Arguments:
- slc: bfloat16 [32, 2, 32, 256], P('acq', None, ('tiles', 'pix')), parts along dimension 2, may hold values from -6 to 6
- disp: bfloat16 [32, 32, 256], P('acq', ('tiles', 'pix')), parts along dimension 1, may hold values from -3 to 3
- times: bfloat16 [32], P('acq'), may hold values from 0 to 4
- velocity: float32 [32, 256], P(('tiles', 'pix')), parts along dimension 0, may hold values from -4 to 4
- amplitude: float32 [32, 256], P(('tiles', 'pix')), parts along dimension 0, may hold values from 0.1 to 1
- pair_ends: int32 [512, 2], P('acq'), may hold values from 0 to 31, as said below
Outputs:
- slc_grad: float32 [32, 2, 32, 256], P('acq', None, ('tiles', 'pix')), parts along dimension 2
- disp_grad: float32 [32, 32, 256], P('acq', ('tiles', 'pix')), parts along dimension 1
The draws below stay inside these ranges and needn't reach their ends.
There are 2 independent parts, one for each index of `tiles`. The reference program is written for one: setup_inputs(seed, part) draws one part's arguments, and reference() takes and returns one part's arrays. A program takes and returns all parts, laid end to end along the dimension named above; an argument that names none is the same for every part. Nothing has to cross between parts.
Inputs may be any that keep to these rules, and one draw needn't show every extreme that they name: `pair_ends`: each row names two different acquisitions. Among the 128 endpoints of one aligned block of 64 rows, at most 16 lie in any run of 4 acquisitions that starts at a multiple of 4, and some run holds exactly 16 in every block.
All inputs are finite; a program needn't handle non-finite values.
Results may differ from the reference program's by a relative error of at most 0.0003.
Values may be sent and summed in bfloat16 or wider, within the bound.
A program may use at most 64 MiB of HBM per device.

```python
import math
import jax
import jax.numpy as jnp
from jax import lax

ACQ_DEV = 4
COLS = 256
PAIR_DEV = 64
LOOK = 2
ACQ = 32
ROWS = 16
PAIRS = 512


def draw_pair_ends(key, part):
    key = jax.random.fold_in(key, 7)
    blocks = PAIRS // PAIR_DEV
    owners = ACQ // ACQ_DEV
    per_side = (PAIR_DEV + owners - 1) // owners

    def one_block(block_key):
        key_ref, key_sec, key_rloc, key_sloc = jax.random.split(block_key, 4)
        ref_owner = jax.random.permutation(key_ref, owners * per_side)[:PAIR_DEV] // per_side
        sec_owner = ref_owner[jax.random.permutation(key_sec, PAIR_DEV)]
        ref_local = jax.random.randint(key_rloc, (PAIR_DEV,), 0, ACQ_DEV)
        sec_local = jax.random.randint(key_sloc, (PAIR_DEV,), 0, ACQ_DEV)
        clash = (sec_owner == ref_owner) & (sec_local == ref_local)
        sec_local = jnp.where(clash, (sec_local + 1) % ACQ_DEV, sec_local)
        return jnp.stack([ref_owner * ACQ_DEV + ref_local, sec_owner * ACQ_DEV + sec_local], 1)
    pairs = jax.vmap(one_block)(jax.random.split(key, blocks))
    return pairs.reshape(PAIRS, 2).astype(jnp.int32)


def level_of(stream_key, shape, pieces, least, top_value):
    def one(axis_at, shards_of):
        draws = jax.random.uniform(jax.random.fold_in(jax.random.fold_in(stream_key, 6), axis_at), (shards_of,), jnp.float32, least / len(pieces), top_value / len(pieces))
        return jnp.repeat(jnp.exp(draws), shape[axis_at] // shards_of).reshape((-1,) + (1,) * (len(shape) - axis_at - 1))

    loudness = one(*pieces[0])
    for cut in pieces[1:]:
        loudness = loudness * one(*cut)
    return loudness


def bell_draw(own_key, extent, spread, bound, pieces=(), held_as=jnp.bfloat16):
    gain = level_of(own_key, extent, pieces, -0.22, 0.18) if pieces else 1.0
    result = jax.random.normal(own_key, extent, jnp.float32) * spread * gain
    return jnp.minimum(jnp.maximum(result, -bound), bound).astype(held_as)


def setup_inputs(seed: int = 0, part: int = 0) -> dict:
    keys = jax.random.split(jax.random.key(seed), 7)
    part_splits = jax.random.split(jax.random.fold_in(keys[6], part), 7)
    return {
        "slc": bell_draw(part_splits[0], (ACQ, 2, ROWS, COLS), 1.0, 6.0, ((0, 8), (2, 2))),
        "disp": jnp.clip(jax.random.uniform(part_splits[1], (ACQ, ROWS, COLS), jnp.float32, -3.0, 3.0) * level_of(part_splits[1], (ACQ, ROWS, COLS), ((0, 8), (1, 2)), -0.4, 0.0), -3.0, 3.0).astype(jnp.bfloat16),
        "times": jnp.clip(4.0 * jax.random.uniform(keys[2], (ACQ,), jnp.float32) ** level_of(keys[2], (ACQ,), ((0, 8),), -0.2, 0.2), 0.0, 4.0).astype(jnp.bfloat16),
        "velocity": bell_draw(part_splits[3], (ROWS, COLS), 1.0, 4.0, ((0, 2),), jnp.float32),
        "amplitude": jnp.clip(jnp.exp(math.log(1.0) - 2.3025851 * jax.random.uniform(part_splits[4], (ROWS, COLS), jnp.float32) ** level_of(part_splits[4], (ROWS, COLS), ((0, 2),), -0.2, 0.2)), 0.1, 1.0),
        "pair_ends": draw_pair_ends(jax.random.fold_in(keys[6], 71), part),
    }


def window_mean(extended, look):
    row_count = extended.shape[-2] - 2 * look
    col_count = extended.shape[-1]
    window = 2 * look + 1
    padded = jnp.pad(extended, [(0, 0)] * (extended.ndim - 1) + [(look, look)])
    summed = jnp.zeros(extended.shape[:-2] + (row_count, col_count), jnp.float32)
    for offset_row in range(window):
        for offset_col in range(window):
            summed = summed + padded[..., offset_row:offset_row + row_count, offset_col:offset_col + col_count]
    return summed / float(window * window)


def residual_of(ref_ext, sec_ext, phase, amplitude, look):
    ref_re, ref_im = ref_ext[:, 0], ref_ext[:, 1]
    sec_re, sec_im = sec_ext[:, 0], sec_ext[:, 1]
    inter = jnp.stack([ref_re * sec_re + ref_im * sec_im, ref_im * sec_re - ref_re * sec_im], 1)
    looked = window_mean(inter, look)
    model_re = jnp.cos(phase)
    model_im = jnp.sin(phase)
    resid = looked - amplitude[None, None] * jnp.stack([model_re, model_im], 1)
    misfit_q = amplitude[None] * (resid[:, 0] * model_im - resid[:, 1] * model_re)
    return resid, misfit_q


def endpoint_terms(adjoint, ref_own, sec_own, misfit_q):
    grad_re, grad_im = adjoint[:, 0], adjoint[:, 1]
    ref_re, ref_im = ref_own[:, 0], ref_own[:, 1]
    sec_re, sec_im = sec_own[:, 0], sec_own[:, 1]
    ref_term = jnp.stack([grad_re * sec_re - grad_im * sec_im, grad_re * sec_im + grad_im * sec_re, -misfit_q], 1)
    sec_term = jnp.stack([grad_re * ref_re + grad_im * ref_im, grad_re * ref_im - grad_im * ref_re, misfit_q], 1)
    return ref_term, sec_term


def reference(slc, disp, times, velocity, amplitude, pair_ends):
    look = LOOK
    z_all = slc.astype(jnp.float32)
    z_ext = jnp.pad(z_all, ((0, 0), (0, 0), (look, look), (0, 0)))
    disp_all = disp.astype(jnp.float32)
    time_all = times.astype(jnp.float32)
    pair_blocks = pair_ends.reshape(PAIRS // PAIR_DEV, PAIR_DEV, 2)

    def accumulate(totals, pair_block):
        grad_z, grad_d = totals
        ref_id = pair_block[:, 0]
        sec_id = pair_block[:, 1]
        phase = (time_all[sec_id] - time_all[ref_id])[:, None, None] * velocity[None] + disp_all[sec_id] - disp_all[ref_id]
        resid, misfit_q = residual_of(z_ext[ref_id], z_ext[sec_id], phase, amplitude, look)
        adjoint = window_mean(jnp.pad(resid, ((0, 0), (0, 0), (look, look), (0, 0))), look)
        ref_term, sec_term = endpoint_terms(adjoint, z_all[ref_id], z_all[sec_id], misfit_q)
        grad_z = grad_z.at[ref_id].add(ref_term[:, :2]).at[sec_id].add(sec_term[:, :2])
        grad_d = grad_d.at[ref_id].add(ref_term[:, 2]).at[sec_id].add(sec_term[:, 2])
        return (grad_z, grad_d), None

    start_z = jnp.zeros(z_all.shape, jnp.float32)
    start_d = jnp.zeros(disp_all.shape, jnp.float32)
    (slc_grad, disp_grad), _ = lax.scan(accumulate, (start_z, start_d), pair_blocks)
    return slc_grad, disp_grad
```

```python
import functools
import math

import jax
import jax.numpy as jnp
from jax import lax
from jax.experimental import pallas as pl
from jax.experimental.pallas import tpu as pltpu
from jax.sharding import PartitionSpec as P

LOOK = 2
GROUP = 2
HALO = 2 * LOOK
LANES = 128
MESH = pl.DeviceIdType.MESH
F32 = jnp.float32
BF16 = jnp.bfloat16
TAU_HI = 6.28125
TAU_LO = 2.0 * math.pi - TAU_HI


def cos_sin(angle):
    turns = jnp.floor(angle * (0.5 / math.pi) + 0.5)
    half = 0.5 * ((angle - turns * TAU_HI) - turns * TAU_LO)
    sq = half * half
    sin_half = jnp.full_like(sq, -1.0 / math.factorial(11))
    for order, sign in ((9, 1.0), (7, -1.0), (5, 1.0), (3, -1.0), (1, 1.0)):
        sin_half = sin_half * sq + sign / math.factorial(order)
    sin_half = sin_half * half
    cos_half = jnp.full_like(sq, 1.0 / math.factorial(12))
    for order, sign in ((10, -1.0), (8, 1.0), (6, -1.0), (4, 1.0), (2, -1.0), (0, 1.0)):
        cos_half = cos_half * sq + sign / math.factorial(order)
    return 1.0 - 2.0 * sin_half * sin_half, 2.0 * sin_half * cos_half


def row_box(values, count):
    pairs = [values[i] + values[i + 1] for i in range(len(values) - 1)]
    out = []
    for i in range(count):
        low = max(0, i - LOOK)
        total, at = None, low
        while at <= i + LOOK:
            if at < i + LOOK:
                piece, at = pairs[at], at + 2
            else:
                piece, at = values[at], at + 1
            total = piece if total is None else total + piece
        out.append(total)
    return out


def put_split(ref, base, values, cols):
    for i in range(0, len(values), 2):
        both = jnp.concatenate([values[i], values[i + 1]], axis=0)
        high = both.astype(BF16)
        low = (both - high.astype(F32)).astype(BF16)
        at = pl.ds(pl.multiple_of(base + 8 * i, 16), 16)
        ref[at, 0:cols] = high
        ref[at, cols : 2 * cols] = low


def kernel(
    n, al, rows, cols, lanes,
    slc_ref, disp_ref, times_ref, vel_ref, amp_ref, ends_ref,
    grad_ref, dgrad_ref,
    rx, oth, msg, msgr, vah, stg, stg_o, zre, zim, ure, uim, velb, ampb,
    zab, aub, band, lhs, filt, acc, qacc, weights,
    msg_send, msg_recv, va_send, va_recv,
    own_send, blk_recv, xf_send, of_send, oth_recv,
):
    me = lax.axis_index("acq")
    pix = lax.axis_index("pix")
    zcount = n // GROUP
    mz = me // GROUP
    mx = me % GROUP
    blk_rows = 3 * al * rows
    slc_rows = 2 * al * rows
    wide = 3 * rows
    ext = rows + HALO
    mid = rows + LOOK
    halves = cols // LANES
    nbr = mz * GROUP + (GROUP - 1 - mx)
    core = {"pix": 1 - pix}

    def peer(step):
        return (me + step) % n

    barrier = pltpu.get_barrier_semaphore()
    for step in range(1, n):
        pl.semaphore_signal(barrier, inc=1, device_id={"acq": peer(step)}, device_id_type=MESH)
    pl.semaphore_signal(barrier, inc=1, device_id=core, device_id_type=MESH)

    rx[me, 0:slc_rows, :] = slc_ref[...]
    rx[me, slc_rows:blk_rows, :] = disp_ref[...]
    count = ends_ref.shape[0]
    first = ends_ref[:, 0:1]
    second = ends_ref[:, 1:2]
    lane = lax.broadcasted_iota(jnp.int32, (count, lanes), 1)
    slot = lax.broadcasted_iota(jnp.int32, (count, 8 * n), 1)

    def spread(ids):
        return (ids // al) * 8 + ids % al

    def hot(where):
        return where.astype(F32).astype(BF16)

    contract = (((0,), (0,)), ((), ()))
    counts = lax.dot_general(
        hot(slot == spread(first)), hot(lane == second), contract, preferred_element_type=F32
    ) + lax.dot_general(
        hot(slot == spread(second)), hot(lane == first), contract, preferred_element_type=F32
    )
    t_lane = lax.broadcasted_iota(jnp.int32, (al, lanes), 1)
    t_sub = lax.broadcasted_iota(jnp.int32, (al, lanes), 0)
    t_row = jnp.sum(jnp.where(t_lane == me * al + t_sub, times_ref[...], 0.0), axis=0, keepdims=True)
    m_sub = lax.broadcasted_iota(jnp.int32, (8, lanes), 0)
    t_tile = jnp.where(m_sub == al, jnp.broadcast_to(t_row, (8, lanes)), 0.0)
    for j in range(n):
        msg[j] = counts[8 * j : 8 * j + 8, :] + t_tile
    msgr[me] = msg[me]

    pl.semaphore_wait(barrier, n)

    def block_copy(src, dst, send_sem, recv_sem, device):
        return pltpu.make_async_remote_copy(
            src_ref=src, dst_ref=dst, send_sem=send_sem, recv_sem=recv_sem,
            device_id=device, device_id_type=MESH,
        )

    def own_copy(step):
        to = ((mz + step) % zcount) * GROUP + mx
        if step == 0:
            to = nbr
        return block_copy(rx.at[me], rx.at[me], own_send.at[step], blk_recv.at[me], {"acq": to})

    def core_copy(j):
        return block_copy(rx.at[j], oth.at[j], of_send.at[j], oth_recv.at[j], core)

    def nbr_copy(j):
        return block_copy(rx.at[j], rx.at[j], xf_send.at[j // GROUP], blk_recv.at[j], {"acq": nbr})

    def msg_copy(step):
        to = peer(step)
        return block_copy(msg.at[to], msgr.at[me], msg_send.at[step], msg_recv.at[me], {"acq": to})

    def va_copy(which):
        src = vel_ref if which == 0 else amp_ref
        return block_copy(src, vah.at[which], va_send.at[which], va_recv.at[which], core)

    for step in range(1, zcount):
        own_copy(step).start()
    own_copy(0).start()
    core_copy(me).start()
    for step in range(1, n):
        msg_copy(step).start()
    va_copy(0).start()
    va_copy(1).start()

    at_row = lax.broadcasted_iota(jnp.int32, (2 * cols, cols), 0) % cols
    at_col = lax.broadcasted_iota(jnp.int32, (2 * cols, cols), 1)
    band[...] = hot(jnp.abs(at_row - at_col) <= LOOK)
    acc[...] = jnp.zeros_like(acc)
    qacc[...] = jnp.zeros_like(qacc)

    def own_row(i):
        return i + pix * (rows - 1 - 2 * i)

    def nbr_row(i):
        place = 2 * rows - 1 - i
        return place + (1 - pix) * (rows - 1 - 2 * place)

    va_copy(0).wait_recv()
    va_copy(1).wait_recv()
    for i in range(mid):
        for which, src, dst in ((0, vel_ref, velb), (1, amp_ref, ampb)):
            if i < rows:
                line = src[pl.ds(own_row(i), 1), :]
            else:
                line = vah[which, pl.ds(nbr_row(i), 1), :]
            dst[8 * i : 8 * i + 8, :] = jnp.broadcast_to(line, (8, cols))

    for step in range(1, n):
        msg_copy(step).wait_send()
        frm = peer(step)
        block_copy(msg.at[frm], msgr.at[frm], msg_send.at[step], msg_recv.at[frm], {"acq": frm}).wait_recv()
    weights[...] = functools.reduce(lambda a, b: a + b, [msgr[j] for j in range(n)])

    def zchunk(k):
        return (mz + k) % zcount

    def forward_column(k):
        j = zchunk(k) * GROUP + mx
        nbr_copy(j).wait_recv()
        nbr_copy(j).start()
        core_copy(j).start()

    def forward_nbr(k):
        j = zchunk(k) * GROUP + (GROUP - 1 - mx)
        nbr_copy(j).wait_recv()
        core_copy(j).start()

    def column_of(row, c):
        l8 = lax.broadcasted_iota(jnp.int32, (8, lanes), 1)
        s8 = lax.broadcasted_iota(jnp.int32, (8, lanes), 0)
        line = jnp.broadcast_to(weights[pl.ds(row, 1), :], (8, lanes))
        return jnp.sum(jnp.where(l8 == c * 8 + s8, line, 0.0), axis=1, keepdims=True)

    def unpack(c):
        for src, dst in ((rx, stg), (oth, stg_o)):
            for s in range(GROUP):
                block = src[c * GROUP + s].astype(F32)
                for h in range(halves):
                    part = block[:, h * LANES : (h + 1) * LANES]
                    for a in range(al):
                        base = (s * al + a) * wide
                        dst[h, base : base + 2 * rows, :] = part[a * 2 * rows : (a + 1) * 2 * rows]
                        dst[h, base + 2 * rows : base + wide, :] = part[
                            slc_rows + a * rows : slc_rows + (a + 1) * rows
                        ]

        def take(i, channel):
            src, row = (stg, own_row(i)) if i < rows else (stg_o, nbr_row(i))
            return jnp.concatenate(
                [src[h, pl.ds(channel * rows + row, 8, stride=wide), :] for h in range(halves)], axis=1
            )

        when = column_of(al, c)
        for i in range(ext):
            zre[8 * i : 8 * i + 8, :] = take(i, 0)
            zim[8 * i : 8 * i + 8, :] = take(i, 1)
            if i < mid:
                u_re, u_im = cos_sin(when * velb[8 * i : 8 * i + 8, :] + take(i, 2))
                ure[8 * i : 8 * i + 8, :] = u_re
                uim[8 * i : 8 * i + 8, :] = u_im

    mean = 1.0 / float((2 * LOOK + 1) ** 2)

    def own_ends():
        def one(a, carry):
            for i in range(ext):
                at = pl.ds(8 * i + al * mx + a, 1)
                for ch, src in ((0, zre), (1, zim)):
                    zab[a, ch, 8 * i : 8 * i + 8, :] = jnp.broadcast_to(src[at, :] * mean, (8, cols))
                if i < mid:
                    for ch, src in ((0, ure), (1, uim)):
                        aub[a, ch, 8 * i : 8 * i + 8, :] = (
                            jnp.broadcast_to(src[at, :], (8, cols)) * ampb[8 * i : 8 * i + 8, :]
                        )
            return carry

        lax.fori_loop(0, al, one, 0)

    def tile(i):
        return slice(8 * i, 8 * i + 8)

    def chunk(k, carry):
        c = zchunk(k)
        forward_nbr(k)

        @pl.when(k + 1 < zcount)
        def _():
            forward_column(k + 1)

        for s in range(GROUP):
            core_copy(c * GROUP + s).wait_recv()
        unpack(c)

        @pl.when(k == 0)
        def _():
            own_ends()

        def inter(a, carry):
            re, im = [], []
            for i in range(ext):
                a_re, a_im = zab[a, 0, tile(i), :], zab[a, 1, tile(i), :]
                b_re, b_im = zre[tile(i), :], zim[tile(i), :]
                re.append(a_re * b_re + a_im * b_im)
                im.append(a_im * b_re - a_re * b_im)
            put_split(lhs, a * (2 * 8 * mid), row_box(re, mid), cols)
            put_split(lhs, a * (2 * 8 * mid) + 8 * mid, row_box(im, mid), cols)
            return carry

        lax.fori_loop(0, al, inter, 0)
        filt[...] = jnp.dot(lhs[...], band[...], preferred_element_type=F32)

        def residual(a, carry):
            weight = column_of(a, c)
            base = a * (2 * 8 * mid)
            re, im = [], []
            for i in range(mid):
                a_re, a_im = aub[a, 0, tile(i), :], aub[a, 1, tile(i), :]
                b_re, b_im = ure[tile(i), :], uim[tile(i), :]
                model_re = b_re * a_re + b_im * a_im
                model_im = b_im * a_re - b_re * a_im
                r_re = filt[pl.ds(pl.multiple_of(base + 8 * i, 8), 8), :] - model_re
                r_im = filt[pl.ds(pl.multiple_of(base + 8 * (mid + i), 8), 8), :] - model_im
                if i < rows:
                    qacc[a, tile(i), :] += weight * (r_re * model_im - r_im * model_re)
                re.append(r_re)
                im.append(r_im)
            put_split(lhs, a * (2 * 8 * rows), row_box(re, rows), cols)
            put_split(lhs, a * (2 * 8 * rows) + 8 * rows, row_box(im, rows), cols)
            return carry

        lax.fori_loop(0, al, residual, 0)
        size = al * 2 * 8 * rows
        filt[0:size, :] = jnp.dot(lhs[0:size, :], band[...], preferred_element_type=F32)

        def gradient(a, carry):
            weight = column_of(a, c) * mean
            base = a * (2 * 8 * rows)
            for i in range(rows):
                g_re = filt[pl.ds(pl.multiple_of(base + 8 * i, 8), 8), :]
                g_im = filt[pl.ds(pl.multiple_of(base + 8 * (rows + i), 8), 8), :]
                b_re, b_im = zre[tile(i), :], zim[tile(i), :]
                acc[a, 0, tile(i), :] += weight * (g_re * b_re - g_im * b_im)
                acc[a, 1, tile(i), :] += weight * (g_re * b_im + g_im * b_re)
            return carry

        lax.fori_loop(0, al, gradient, 0)
        return carry

    lax.fori_loop(0, zcount, chunk, 0)

    def finish(a, carry):
        for i in range(rows):
            row = pl.ds(own_row(i), 1)
            for ch in range(2):
                grad_ref[a, ch, row, :] = jnp.sum(acc[a, ch, tile(i), :], axis=0, keepdims=True)
            dgrad_ref[a, row, :] = -jnp.sum(qacc[a, tile(i), :], axis=0, keepdims=True)
        return carry

    lax.fori_loop(0, al, finish, 0)

    for step in range(zcount):
        own_copy(step).wait_send()
    va_copy(0).wait_send()
    va_copy(1).wait_send()

    def drain(j, carry):
        core_copy(j).wait_send()
        return carry

    lax.fori_loop(0, n, drain, 0)

    def drain_nbr(k, carry):
        nbr_copy(zchunk(k) * GROUP + mx).wait_send()
        return carry

    lax.fori_loop(1, zcount, drain_nbr, 0)


def per_device(slc, disp, times, velocity, amplitude, pair_ends):
    al, _, rows, cols = slc.shape
    n = lax.axis_size("acq")
    lanes = -(-(al * n) // LANES) * LANES
    ext, mid = rows + HALO, rows + LOOK
    zcount = n // GROUP
    vmem = pl.BlockSpec(memory_space=pltpu.VMEM)
    dma = pltpu.SemaphoreType.DMA
    scratch = [
        pltpu.VMEM((n, 3 * al * rows, cols), BF16),
        pltpu.VMEM((n, 3 * al * rows, cols), BF16),
        pltpu.VMEM((n, 8, lanes), F32),
        pltpu.VMEM((n, 8, lanes), F32),
        pltpu.VMEM((2, rows, cols), F32),
        pltpu.VMEM((cols // LANES, 8 * 3 * rows, LANES), F32),
        pltpu.VMEM((cols // LANES, 8 * 3 * rows, LANES), F32),
        pltpu.VMEM((8 * ext, cols), F32),
        pltpu.VMEM((8 * ext, cols), F32),
        pltpu.VMEM((8 * mid, cols), F32),
        pltpu.VMEM((8 * mid, cols), F32),
        pltpu.VMEM((8 * mid, cols), F32),
        pltpu.VMEM((8 * mid, cols), F32),
        pltpu.VMEM((al, 2, 8 * ext, cols), F32),
        pltpu.VMEM((al, 2, 8 * mid, cols), F32),
        pltpu.VMEM((2 * cols, cols), BF16),
        pltpu.VMEM((al * 2 * 8 * mid, 2 * cols), BF16),
        pltpu.VMEM((al * 2 * 8 * mid, cols), F32),
        pltpu.VMEM((al, 2, 8 * rows, cols), F32),
        pltpu.VMEM((al, 8 * rows, cols), F32),
        pltpu.VMEM((8, lanes), F32),
        dma((n,)), dma((n,)), dma((2,)), dma((2,)),
        dma((zcount,)), dma((n,)), dma((zcount,)), dma((n,)), dma((n,)),
    ]
    t_wide = jnp.broadcast_to(times.astype(F32)[:, None], (al, lanes))
    return pl.pallas_call(
        functools.partial(kernel, n, al, rows, cols, lanes),
        out_shape=(
            jax.ShapeDtypeStruct((al, 2, rows, cols), F32),
            jax.ShapeDtypeStruct((al, rows, cols), F32),
        ),
        in_specs=[vmem] * 6,
        out_specs=(vmem, vmem),
        scratch_shapes=scratch,
        compiler_params=pltpu.CompilerParams(
            collective_id=0, has_side_effects=True, vmem_limit_bytes=40 * 1024 * 1024
        ),
    )(
        slc.reshape(2 * al * rows, cols),
        disp.reshape(al * rows, cols),
        t_wide, velocity, amplitude, pair_ends,
    )


def solution(mesh):
    return jax.shard_map(
        per_device,
        mesh=mesh,
        in_specs=(
            P("acq", None, ("tiles", "pix"), None),
            P("acq", ("tiles", "pix"), None),
            P("acq"),
            P(("tiles", "pix"), None),
            P(("tiles", "pix"), None),
            P("acq", None),
        ),
        out_specs=(P("acq", None, ("tiles", "pix"), None), P("acq", ("tiles", "pix"), None)),
        check_vma=False,
    )
```

```python
import functools
import math

import jax
import jax.numpy as jnp
from jax import lax
from jax.experimental import pallas as pl
from jax.experimental.pallas import tpu as pltpu
from jax.sharding import PartitionSpec as P

LOOK = 2
GROUP = 2
HALO = 2 * LOOK
LANES = 128
MESH = pl.DeviceIdType.MESH
F32 = jnp.float32
BF16 = jnp.bfloat16
TAU_HI = 6.28125
TAU_LO = 2.0 * math.pi - TAU_HI


def cos_sin(angle):
    turns = jnp.floor(angle * (0.5 / math.pi) + 0.5)
    half = 0.5 * ((angle - turns * TAU_HI) - turns * TAU_LO)
    sq = half * half
    sin_half = jnp.full_like(sq, -1.0 / math.factorial(11))
    for order, sign in ((9, 1.0), (7, -1.0), (5, 1.0), (3, -1.0), (1, 1.0)):
        sin_half = sin_half * sq + sign / math.factorial(order)
    sin_half = sin_half * half
    cos_half = jnp.full_like(sq, 1.0 / math.factorial(12))
    for order, sign in ((10, -1.0), (8, 1.0), (6, -1.0), (4, 1.0), (2, -1.0), (0, 1.0)):
        cos_half = cos_half * sq + sign / math.factorial(order)
    return 1.0 - 2.0 * sin_half * sin_half, 2.0 * sin_half * cos_half


def row_box(values, count):
    pairs = [values[i] + values[i + 1] for i in range(len(values) - 1)]
    out = []
    for i in range(count):
        low = max(0, i - LOOK)
        total, at = None, low
        while at <= i + LOOK:
            if at < i + LOOK:
                piece, at = pairs[at], at + 2
            else:
                piece, at = values[at], at + 1
            total = piece if total is None else total + piece
        out.append(total)
    return out


def put_split(ref, base, values, cols):
    for i in range(0, len(values), 2):
        both = jnp.concatenate([values[i], values[i + 1]], axis=0)
        high = both.astype(BF16)
        low = (both - high.astype(F32)).astype(BF16)
        at = pl.ds(pl.multiple_of(base + 8 * i, 16), 16)
        ref[at, 0:cols] = high
        ref[at, cols : 2 * cols] = low


def kernel(
    n, al, rows, cols, lanes,
    slc_in, disp_in, times_ref, vel_in, amp_in, ends_in,
    grad_ref, dgrad_ref,
    rx, oth, msg, msgr, vah, stg, stg_o, zre, zim, ure, uim, velb, ampb,
    zab, aub, band, lhs, filt, lhs2, filt2, acc, qacc, weights,
    msg_send, msg_recv, va_send, va_recv,
    own_send, blk_recv, of_send, oth_recv,
    vel_ref, amp_ref, ends_ref, in_sem,
):
    me = lax.axis_index("acq")
    pix = lax.axis_index("pix")
    zcount = n // GROUP
    mz = me // GROUP
    mx = me % GROUP
    blk_rows = 3 * al * rows
    slc_rows = 2 * al * rows
    wide = 3 * rows
    ext = rows + HALO
    mid = rows + LOOK
    halves = cols // LANES
    core = {"pix": 1 - pix}

    def peer(step):
        return (me + step) % n

    loads = [
        pltpu.make_async_copy(src, dst, in_sem.at[i])
        for i, (src, dst) in enumerate((
            (ends_in, ends_ref),
            (slc_in, rx.at[me, 0:slc_rows, :]),
            (disp_in, rx.at[me, slc_rows:blk_rows, :]),
            (vel_in, vel_ref),
            (amp_in, amp_ref),
        ))
    ]
    for load in loads:
        load.start()

    barrier = pltpu.get_barrier_semaphore()
    for step in range(1, n):
        pl.semaphore_signal(barrier, inc=1, device_id={"acq": peer(step)}, device_id_type=MESH)
    pl.semaphore_signal(barrier, inc=1, device_id=core, device_id_type=MESH)

    loads[0].wait()
    count = ends_ref.shape[1]
    first = ends_ref[0:1, :]
    second = ends_ref[1:2, :]
    lane = lax.broadcasted_iota(jnp.int32, (lanes, count), 0)
    slot = lax.broadcasted_iota(jnp.int32, (8 * n, count), 0)

    def spread(ids):
        return (ids // al) * 8 + ids % al

    def hot(where):
        return where.astype(F32).astype(BF16)

    contract = (((1,), (1,)), ((), ()))
    counts = lax.dot_general(
        hot(slot == spread(first)), hot(lane == second), contract, preferred_element_type=F32
    ) + lax.dot_general(
        hot(slot == spread(second)), hot(lane == first), contract, preferred_element_type=F32
    )
    t_lane = lax.broadcasted_iota(jnp.int32, (al, lanes), 1)
    t_sub = lax.broadcasted_iota(jnp.int32, (al, lanes), 0)
    t_row = jnp.sum(jnp.where(t_lane == me * al + t_sub, times_ref[...], 0.0), axis=0, keepdims=True)
    m_sub = lax.broadcasted_iota(jnp.int32, (8, lanes), 0)
    t_tile = jnp.where(m_sub == al, jnp.broadcast_to(t_row, (8, lanes)), 0.0)
    for j in range(n):
        msg[j] = counts[8 * j : 8 * j + 8, :] + t_tile
    msgr[me] = msg[me]

    for load in loads[1:]:
        load.wait()
    pl.semaphore_wait(barrier, n)

    def block_copy(src, dst, send_sem, recv_sem, device):
        return pltpu.make_async_remote_copy(
            src_ref=src, dst_ref=dst, send_sem=send_sem, recv_sem=recv_sem,
            device_id=device, device_id_type=MESH,
        )

    def own_copy(step):
        to = ((mz + step // GROUP) % zcount) * GROUP + (mx + step) % GROUP
        return block_copy(rx.at[me], rx.at[me], own_send.at[step], blk_recv.at[me], {"acq": to})

    def core_copy(j):
        return block_copy(rx.at[j], oth.at[j], of_send.at[j], oth_recv.at[j], core)

    def msg_copy(step):
        to = peer(step)
        return block_copy(msg.at[to], msgr.at[me], msg_send.at[step], msg_recv.at[me], {"acq": to})

    def va_copy(which):
        src = vel_ref if which == 0 else amp_ref
        return block_copy(src, vah.at[which], va_send.at[which], va_recv.at[which], core)

    for step in range(1, n):
        msg_copy(step).start()
    for step in range(1, n):
        own_copy(step).start()
    va_copy(0).start()
    va_copy(1).start()
    core_copy(me).start()

    at_row = lax.broadcasted_iota(jnp.int32, (2 * cols, cols), 0) % cols
    at_col = lax.broadcasted_iota(jnp.int32, (2 * cols, cols), 1)
    band[...] = hot(jnp.abs(at_row - at_col) <= LOOK)
    acc[...] = jnp.zeros_like(acc)
    qacc[...] = jnp.zeros_like(qacc)

    def own_row(i):
        return i + pix * (rows - 1 - 2 * i)

    def nbr_row(i):
        place = 2 * rows - 1 - i
        return place + (1 - pix) * (rows - 1 - 2 * place)

    va_copy(0).wait_recv()
    va_copy(1).wait_recv()
    for i in range(mid):
        for which, src, dst in ((0, vel_ref, velb), (1, amp_ref, ampb)):
            if i < rows:
                line = src[pl.ds(own_row(i), 1), :]
            else:
                line = vah[which, pl.ds(nbr_row(i), 1), :]
            dst[8 * i : 8 * i + 8, :] = jnp.broadcast_to(line, (8, cols))

    for step in range(1, n):
        msg_copy(step).wait_send()
        frm = peer(step)
        block_copy(msg.at[frm], msgr.at[frm], msg_send.at[step], msg_recv.at[frm], {"acq": frm}).wait_recv()
    weights[...] = functools.reduce(lambda a, b: a + b, [msgr[j] for j in range(n)])

    def zchunk(k):
        return (mz + k) % zcount

    def forward(k, s):
        j = zchunk(k) * GROUP + (mx + s) % GROUP
        block_copy(rx.at[j], rx.at[j], own_send.at[0], blk_recv.at[j], {"acq": j}).wait_recv()
        core_copy(j).start()

    def column_of(row, c):
        l8 = lax.broadcasted_iota(jnp.int32, (8, lanes), 1)
        s8 = lax.broadcasted_iota(jnp.int32, (8, lanes), 0)
        line = jnp.broadcast_to(weights[pl.ds(row, 1), :], (8, lanes))
        return jnp.sum(jnp.where(l8 == c * 8 + s8, line, 0.0), axis=1, keepdims=True)

    def unpack(c):
        for src, dst in ((rx, stg), (oth, stg_o)):
            for s in range(GROUP):
                block = src[c * GROUP + s].astype(F32)
                for h in range(halves):
                    part = block[:, h * LANES : (h + 1) * LANES]
                    for a in range(al):
                        base = (s * al + a) * wide
                        dst[h, base : base + 2 * rows, :] = part[a * 2 * rows : (a + 1) * 2 * rows]
                        dst[h, base + 2 * rows : base + wide, :] = part[
                            slc_rows + a * rows : slc_rows + (a + 1) * rows
                        ]

        def take(i, channel):
            src, row = (stg, own_row(i)) if i < rows else (stg_o, nbr_row(i))
            return jnp.concatenate(
                [src[h, pl.ds(channel * rows + row, 8, stride=wide), :] for h in range(halves)], axis=1
            )

        when = column_of(al, c)
        for i in range(ext):
            zre[8 * i : 8 * i + 8, :] = take(i, 0)
            zim[8 * i : 8 * i + 8, :] = take(i, 1)
            if i < mid:
                u_re, u_im = cos_sin(when * velb[8 * i : 8 * i + 8, :] + take(i, 2))
                ure[8 * i : 8 * i + 8, :] = u_re
                uim[8 * i : 8 * i + 8, :] = u_im

    mean = 1.0 / float((2 * LOOK + 1) ** 2)

    def own_ends():
        def one(a, carry):
            for i in range(ext):
                at = pl.ds(8 * i + al * mx + a, 1)
                for ch, src in ((0, zre), (1, zim)):
                    zab[a, ch, 8 * i : 8 * i + 8, :] = jnp.broadcast_to(src[at, :] * mean, (8, cols))
                if i < mid:
                    for ch, src in ((0, ure), (1, uim)):
                        aub[a, ch, 8 * i : 8 * i + 8, :] = (
                            jnp.broadcast_to(src[at, :], (8, cols)) * ampb[8 * i : 8 * i + 8, :]
                        )
            return carry

        lax.fori_loop(0, al, one, 0)

    def columns(src, span):
        return jnp.dot(src[span, :], band[...], preferred_element_type=F32)

    def tile(i):
        return slice(8 * i, 8 * i + 8)

    def chunk(k, carry):
        c = zchunk(k)

        @pl.when(k > 0)
        def _():
            forward(k, 0)

        forward(k, 1)
        for s in range(GROUP):
            core_copy(c * GROUP + s).wait_recv()
        unpack(c)

        @pl.when(k == 0)
        def _():
            own_ends()

        def one(a, carry):
            weight = jnp.broadcast_to(column_of(a, c), (8, cols))
            base = a * (2 * 8 * mid)
            re, im = [], []
            for i in range(ext):
                a_re, a_im = zab[a, 0, tile(i), :], zab[a, 1, tile(i), :]
                b_re, b_im = zre[tile(i), :], zim[tile(i), :]
                re.append(a_re * b_re + a_im * b_im)
                im.append(a_im * b_re - a_re * b_im)
            put_split(lhs, base, row_box(re, mid), cols)
            put_split(lhs, base + 8 * mid, row_box(im, mid), cols)
            span = pl.ds(pl.multiple_of(base, 16), 2 * 8 * mid)
            filt[span, :] = columns(lhs, span)

            re, im = [], []
            for i in range(mid):
                a_re, a_im = aub[a, 0, tile(i), :], aub[a, 1, tile(i), :]
                b_re, b_im = ure[tile(i), :], uim[tile(i), :]
                model_re = b_re * a_re + b_im * a_im
                model_im = b_im * a_re - b_re * a_im
                r_re = filt[pl.ds(pl.multiple_of(base + 8 * i, 8), 8), :] - model_re
                r_im = filt[pl.ds(pl.multiple_of(base + 8 * (mid + i), 8), 8), :] - model_im
                if i < rows:
                    qacc[a, tile(i), :] += weight * (r_re * model_im - r_im * model_re)
                re.append(r_re)
                im.append(r_im)
            base = a * (2 * 8 * rows)
            put_split(lhs2, base, row_box(re, rows), cols)
            put_split(lhs2, base + 8 * rows, row_box(im, rows), cols)
            span = pl.ds(pl.multiple_of(base, 16), 2 * 8 * rows)
            filt2[span, :] = columns(lhs2, span)

            weight = weight * mean
            for i in range(rows):
                g_re = filt2[pl.ds(pl.multiple_of(base + 8 * i, 8), 8), :]
                g_im = filt2[pl.ds(pl.multiple_of(base + 8 * (rows + i), 8), 8), :]
                b_re, b_im = zre[tile(i), :], zim[tile(i), :]
                acc[a, 0, tile(i), :] += weight * (g_re * b_re - g_im * b_im)
                acc[a, 1, tile(i), :] += weight * (g_re * b_im + g_im * b_re)
            return carry

        lax.fori_loop(0, al, one, 0, unroll=True)
        return carry

    lax.fori_loop(0, zcount, chunk, 0)

    def finish(a, carry):
        for i in range(rows):
            row = pl.ds(own_row(i), 1)
            for ch in range(2):
                grad_ref[a, ch, row, :] = jnp.sum(acc[a, ch, tile(i), :], axis=0, keepdims=True)
            dgrad_ref[a, row, :] = -jnp.sum(qacc[a, tile(i), :], axis=0, keepdims=True)
        return carry

    lax.fori_loop(0, al, finish, 0)

    for step in range(1, n):
        own_copy(step).wait_send()
    va_copy(0).wait_send()
    va_copy(1).wait_send()

    def drain(j, carry):
        core_copy(j).wait_send()
        return carry

    lax.fori_loop(0, n, drain, 0)


def per_device(slc, disp, times, velocity, amplitude, pair_ends):
    al, _, rows, cols = slc.shape
    n = lax.axis_size("acq")
    lanes = -(-(al * n) // LANES) * LANES
    ext, mid = rows + HALO, rows + LOOK
    zcount = n // GROUP
    vmem = pl.BlockSpec(memory_space=pltpu.VMEM)
    dma = pltpu.SemaphoreType.DMA
    scratch = [
        pltpu.VMEM((n, 3 * al * rows, cols), BF16),
        pltpu.VMEM((n, 3 * al * rows, cols), BF16),
        pltpu.VMEM((n, 8, lanes), F32),
        pltpu.VMEM((n, 8, lanes), F32),
        pltpu.VMEM((2, rows, cols), F32),
        pltpu.VMEM((cols // LANES, 8 * 3 * rows, LANES), F32),
        pltpu.VMEM((cols // LANES, 8 * 3 * rows, LANES), F32),
        pltpu.VMEM((8 * ext, cols), F32),
        pltpu.VMEM((8 * ext, cols), F32),
        pltpu.VMEM((8 * mid, cols), F32),
        pltpu.VMEM((8 * mid, cols), F32),
        pltpu.VMEM((8 * mid, cols), F32),
        pltpu.VMEM((8 * mid, cols), F32),
        pltpu.VMEM((al, 2, 8 * ext, cols), F32),
        pltpu.VMEM((al, 2, 8 * mid, cols), F32),
        pltpu.VMEM((2 * cols, cols), BF16),
        pltpu.VMEM((al * 2 * 8 * mid, 2 * cols), BF16),
        pltpu.VMEM((al * 2 * 8 * mid, cols), F32),
        pltpu.VMEM((al * 2 * 8 * rows, 2 * cols), BF16),
        pltpu.VMEM((al * 2 * 8 * rows, cols), F32),
        pltpu.VMEM((al, 2, 8 * rows, cols), F32),
        pltpu.VMEM((al, 8 * rows, cols), F32),
        pltpu.VMEM((8, lanes), F32),
        dma((n,)), dma((n,)), dma((2,)), dma((2,)),
        dma((n,)), dma((n,)), dma((n,)), dma((n,)),
        pltpu.VMEM((rows, cols), F32),
        pltpu.VMEM((rows, cols), F32),
        pltpu.VMEM(pair_ends.shape[::-1], jnp.int32),
        dma((5,)),
    ]
    hbm = pl.BlockSpec(memory_space=pltpu.HBM)
    t_wide = jnp.broadcast_to(times.astype(F32)[:, None], (al, lanes))
    return pl.pallas_call(
        functools.partial(kernel, n, al, rows, cols, lanes),
        out_shape=(
            jax.ShapeDtypeStruct((al, 2, rows, cols), F32),
            jax.ShapeDtypeStruct((al, rows, cols), F32),
        ),
        in_specs=[hbm, hbm, vmem, hbm, hbm, hbm],
        out_specs=(vmem, vmem),
        scratch_shapes=scratch,
        compiler_params=pltpu.CompilerParams(
            collective_id=0, has_side_effects=True, vmem_limit_bytes=63 * 1024 * 1024
        ),
    )(
        slc.reshape(2 * al * rows, cols),
        disp.reshape(al * rows, cols),
        t_wide, velocity, amplitude, pair_ends.T,
    )


def solution(mesh):
    return jax.shard_map(
        per_device,
        mesh=mesh,
        in_specs=(
            P("acq", None, ("tiles", "pix"), None),
            P("acq", ("tiles", "pix"), None),
            P("acq"),
            P(("tiles", "pix"), None),
            P(("tiles", "pix"), None),
            P("acq", None),
        ),
        out_specs=(P("acq", None, ("tiles", "pix"), None), P("acq", ("tiles", "pix"), None)),
        check_vma=False,
    )
```

```python
import functools
import math

import jax
import jax.numpy as jnp
from jax import lax
from jax.experimental import pallas as pl
from jax.experimental.pallas import tpu as pltpu
from jax.sharding import PartitionSpec as P

LOOK = 2
GROUP = 2
HALO = 2 * LOOK
LANES = 128
MESH = pl.DeviceIdType.MESH
F32 = jnp.float32
BF16 = jnp.bfloat16
TAU_HI = 6.28125
TAU_LO = 2.0 * math.pi - TAU_HI


def cos_sin(angle):
    turns = jnp.floor(angle * (0.5 / math.pi) + 0.5)
    half = 0.5 * ((angle - turns * TAU_HI) - turns * TAU_LO)
    sq = half * half
    sin_half = jnp.full_like(sq, -1.0 / math.factorial(11))
    for order, sign in ((9, 1.0), (7, -1.0), (5, 1.0), (3, -1.0), (1, 1.0)):
        sin_half = sin_half * sq + sign / math.factorial(order)
    sin_half = sin_half * half
    cos_half = jnp.full_like(sq, 1.0 / math.factorial(12))
    for order, sign in ((10, -1.0), (8, 1.0), (6, -1.0), (4, 1.0), (2, -1.0), (0, 1.0)):
        cos_half = cos_half * sq + sign / math.factorial(order)
    return 1.0 - 2.0 * sin_half * sin_half, 2.0 * sin_half * cos_half


def row_box(values, count):
    pairs = [values[i] + values[i + 1] for i in range(len(values) - 1)]
    out = []
    for i in range(count):
        low = max(0, i - LOOK)
        total, at = None, low
        while at <= i + LOOK:
            if at < i + LOOK:
                piece, at = pairs[at], at + 2
            else:
                piece, at = values[at], at + 1
            total = piece if total is None else total + piece
        out.append(total)
    return out


def put_split(ref, base, values, cols):
    for i in range(0, len(values), 2):
        both = jnp.concatenate([values[i], values[i + 1]], axis=0)
        high = both.astype(BF16)
        low = (both - high.astype(F32)).astype(BF16)
        at = pl.ds(pl.multiple_of(base + 8 * i, 16), 16)
        ref[at, 0:cols] = high
        ref[at, cols : 2 * cols] = low


def kernel(
    n, al, rows, cols, lanes,
    slc_in, disp_in, times_ref, vel_in, amp_in, ends_in,
    grad_ref, dgrad_ref,
    rx, oth, msg, msgr, vah, stg, stg_o, zre, zim, ure, uim, velb, ampb,
    zab, aub, band, lhs, filt, lhs2, filt2, acc, qacc, weights,
    msg_send, msg_recv, va_send, va_recv,
    own_send, blk_recv, of_send, oth_recv,
    vel_ref, amp_ref, ends_ref, t_tile, in_sem,
):
    me = lax.axis_index("acq")
    pix = lax.axis_index("pix")
    zcount = n // GROUP
    mz = me // GROUP
    mx = me % GROUP
    blk_rows = 3 * al * rows
    slc_rows = 2 * al * rows
    wide = 3 * rows
    ext = rows + HALO
    mid = rows + LOOK
    halves = cols // LANES
    core = {"pix": 1 - pix}

    def peer(step):
        return (me + step) % n

    def zchunk(k):
        return mz ^ k

    loads = [
        pltpu.make_async_copy(src, dst, in_sem.at[i])
        for i, (src, dst) in enumerate((
            (ends_in, ends_ref),
            (slc_in, rx.at[me, 0:slc_rows, :]),
            (disp_in, rx.at[me, slc_rows:blk_rows, :]),
            (vel_in, vel_ref),
            (amp_in, amp_ref),
        ))
    ]
    for load in loads:
        load.start()

    barrier = pltpu.get_barrier_semaphore()
    for step in range(1, n):
        pl.semaphore_signal(barrier, inc=1, device_id={"acq": peer(step)}, device_id_type=MESH)
    pl.semaphore_signal(barrier, inc=1, device_id=core, device_id_type=MESH)

    loads[0].wait()
    count = ends_ref.shape[1]
    first = ends_ref[0:1, :]
    second = ends_ref[1:2, :]
    lane = lax.broadcasted_iota(jnp.int32, (lanes, count), 0)
    slot = lax.broadcasted_iota(jnp.int32, (8 * n, count), 0)

    def spread(ids):
        return (ids // al) * 8 + ids % al

    def hot(where):
        return where.astype(F32).astype(BF16)

    contract = (((1,), (1,)), ((), ()))
    counts = lax.dot_general(
        hot(slot == spread(first)), hot(lane == second), contract, preferred_element_type=F32
    ) + lax.dot_general(
        hot(slot == spread(second)), hot(lane == first), contract, preferred_element_type=F32
    )
    t_tile[...] = jnp.zeros_like(t_tile)
    t_tile[al : al + 1, 0:al] = times_ref[...].astype(F32)
    for j in range(n):
        msg[j] = counts[8 * j : 8 * j + 8, :] + t_tile[...]
    msgr[me] = msg[me]

    for load in loads[1:]:
        load.wait()
    pl.semaphore_wait(barrier, n)

    def block_copy(src, dst, send_sem, recv_sem, device):
        return pltpu.make_async_remote_copy(
            src_ref=src, dst_ref=dst, send_sem=send_sem, recv_sem=recv_sem,
            device_id=device, device_id_type=MESH,
        )

    def own_copy(step):
        to = zchunk(step // GROUP) * GROUP + (mx + step) % GROUP
        return block_copy(rx.at[me], rx.at[me], own_send.at[step], blk_recv.at[me], {"acq": to})

    def core_copy(j):
        return block_copy(rx.at[j], oth.at[j], of_send.at[j], oth_recv.at[j], core)

    def msg_copy(step):
        to = peer(step)
        return block_copy(msg.at[to], msgr.at[me], msg_send.at[step], msg_recv.at[me], {"acq": to})

    def va_copy(which):
        src = vel_ref if which == 0 else amp_ref
        return block_copy(src, vah.at[which], va_send.at[which], va_recv.at[which], core)

    for step in range(1, n):
        msg_copy(step).start()
    for step in range(1, n):
        own_copy(step).start()
    va_copy(0).start()
    va_copy(1).start()
    core_copy(me).start()

    at_row = lax.broadcasted_iota(jnp.int32, (2 * cols, cols), 0) % cols
    at_col = lax.broadcasted_iota(jnp.int32, (2 * cols, cols), 1)
    band[...] = hot(jnp.abs(at_row - at_col) <= LOOK)
    acc[...] = jnp.zeros_like(acc)
    qacc[...] = jnp.zeros_like(qacc)

    def own_row(i):
        return i + pix * (rows - 1 - 2 * i)

    def nbr_row(i):
        place = 2 * rows - 1 - i
        return place + (1 - pix) * (rows - 1 - 2 * place)

    va_copy(0).wait_recv()
    va_copy(1).wait_recv()
    for i in range(mid):
        for which, src, dst in ((0, vel_ref, velb), (1, amp_ref, ampb)):
            if i < rows:
                line = src[pl.ds(own_row(i), 1), :]
            else:
                line = vah[which, pl.ds(nbr_row(i), 1), :]
            dst[8 * i : 8 * i + 8, :] = jnp.broadcast_to(line, (8, cols))

    for step in range(1, n):
        msg_copy(step).wait_send()
        frm = peer(step)
        block_copy(msg.at[frm], msgr.at[frm], msg_send.at[step], msg_recv.at[frm], {"acq": frm}).wait_recv()
    weights[...] = functools.reduce(lambda a, b: a + b, [msgr[j] for j in range(n)])

    def forward(k, s):
        j = zchunk(k) * GROUP + (mx + s) % GROUP
        block_copy(rx.at[j], rx.at[j], own_send.at[0], blk_recv.at[j], {"acq": j}).wait_recv()
        core_copy(j).start()

    def column_of(row, c):
        l8 = lax.broadcasted_iota(jnp.int32, (8, lanes), 1)
        s8 = lax.broadcasted_iota(jnp.int32, (8, lanes), 0)
        line = jnp.broadcast_to(weights[pl.ds(row, 1), :], (8, lanes))
        return jnp.sum(jnp.where(l8 == c * 8 + s8, line, 0.0), axis=1, keepdims=True)

    def unpack(c):
        for src, dst in ((rx, stg), (oth, stg_o)):
            for s in range(GROUP):
                block = src[c * GROUP + s].astype(F32)
                for h in range(halves):
                    part = block[:, h * LANES : (h + 1) * LANES]
                    for a in range(al):
                        base = (s * al + a) * wide
                        dst[h, base : base + 2 * rows, :] = part[a * 2 * rows : (a + 1) * 2 * rows]
                        dst[h, base + 2 * rows : base + wide, :] = part[
                            slc_rows + a * rows : slc_rows + (a + 1) * rows
                        ]

        def take(i, channel):
            src, row = (stg, own_row(i)) if i < rows else (stg_o, nbr_row(i))
            return jnp.concatenate(
                [src[h, pl.ds(channel * rows + row, 8, stride=wide), :] for h in range(halves)], axis=1
            )

        t_lane = lax.broadcasted_iota(jnp.int32, (8, lanes), 1)
        t_sub = lax.broadcasted_iota(jnp.int32, (8, lanes), 0)
        t_line = jnp.where(
            t_sub < al,
            jnp.broadcast_to(msgr[c * GROUP, al : al + 1, :], (8, lanes)),
            jnp.broadcast_to(msgr[c * GROUP + 1, al : al + 1, :], (8, lanes)),
        )
        when = jnp.sum(jnp.where(t_lane == t_sub % al, t_line, 0.0), axis=1, keepdims=True)
        for i in range(ext):
            zre[8 * i : 8 * i + 8, :] = take(i, 0)
            zim[8 * i : 8 * i + 8, :] = take(i, 1)
            if i < mid:
                u_re, u_im = cos_sin(when * velb[8 * i : 8 * i + 8, :] + take(i, 2))
                ure[8 * i : 8 * i + 8, :] = u_re
                uim[8 * i : 8 * i + 8, :] = u_im

    mean = 1.0 / float((2 * LOOK + 1) ** 2)

    def own_ends():
        def one(a, carry):
            for i in range(ext):
                at = pl.ds(8 * i + al * mx + a, 1)
                for ch, src in ((0, zre), (1, zim)):
                    zab[a, ch, 8 * i : 8 * i + 8, :] = jnp.broadcast_to(src[at, :] * mean, (8, cols))
                if i < mid:
                    for ch, src in ((0, ure), (1, uim)):
                        aub[a, ch, 8 * i : 8 * i + 8, :] = (
                            jnp.broadcast_to(src[at, :], (8, cols)) * ampb[8 * i : 8 * i + 8, :]
                        )
            return carry

        lax.fori_loop(0, al, one, 0)

    def columns(src, span):
        return jnp.dot(src[span, :], band[...], preferred_element_type=F32)

    def tile(i):
        return slice(8 * i, 8 * i + 8)

    def chunk(k, carry):
        c = zchunk(k)

        @pl.when(k > 0)
        def _():
            forward(k, 0)

        forward(k, 1)
        for s in range(GROUP):
            core_copy(c * GROUP + s).wait_recv()
        unpack(c)

        @pl.when(k == 0)
        def _():
            own_ends()

        def one(a, carry):
            weight = jnp.broadcast_to(column_of(a, c), (8, cols))
            base = a * (2 * 8 * mid)
            re, im = [], []
            for i in range(ext):
                a_re, a_im = zab[a, 0, tile(i), :], zab[a, 1, tile(i), :]
                b_re, b_im = zre[tile(i), :], zim[tile(i), :]
                re.append(a_re * b_re + a_im * b_im)
                im.append(a_im * b_re - a_re * b_im)
            put_split(lhs, base, row_box(re, mid), cols)
            put_split(lhs, base + 8 * mid, row_box(im, mid), cols)
            span = pl.ds(pl.multiple_of(base, 16), 2 * 8 * mid)
            filt[span, :] = columns(lhs, span)

            re, im = [], []
            for i in range(mid):
                a_re, a_im = aub[a, 0, tile(i), :], aub[a, 1, tile(i), :]
                b_re, b_im = ure[tile(i), :], uim[tile(i), :]
                model_re = b_re * a_re + b_im * a_im
                model_im = b_im * a_re - b_re * a_im
                r_re = filt[pl.ds(pl.multiple_of(base + 8 * i, 8), 8), :] - model_re
                r_im = filt[pl.ds(pl.multiple_of(base + 8 * (mid + i), 8), 8), :] - model_im
                if i < rows:
                    qacc[a, tile(i), :] += weight * (r_re * model_im - r_im * model_re)
                re.append(r_re)
                im.append(r_im)
            base = a * (2 * 8 * rows)
            put_split(lhs2, base, row_box(re, rows), cols)
            put_split(lhs2, base + 8 * rows, row_box(im, rows), cols)
            span = pl.ds(pl.multiple_of(base, 16), 2 * 8 * rows)
            filt2[span, :] = columns(lhs2, span)

            weight = weight * mean
            for i in range(rows):
                g_re = filt2[pl.ds(pl.multiple_of(base + 8 * i, 8), 8), :]
                g_im = filt2[pl.ds(pl.multiple_of(base + 8 * (rows + i), 8), 8), :]
                b_re, b_im = zre[tile(i), :], zim[tile(i), :]
                acc[a, 0, tile(i), :] += weight * (g_re * b_re - g_im * b_im)
                acc[a, 1, tile(i), :] += weight * (g_re * b_im + g_im * b_re)
            return carry

        lax.fori_loop(0, al, one, 0, unroll=True)
        return carry

    lax.fori_loop(0, zcount, chunk, 0)

    def finish(a, carry):
        for i in range(rows):
            row = pl.ds(own_row(i), 1)
            for ch in range(2):
                grad_ref[a, ch, row, :] = jnp.sum(acc[a, ch, tile(i), :], axis=0, keepdims=True)
            dgrad_ref[a, row, :] = -jnp.sum(qacc[a, tile(i), :], axis=0, keepdims=True)
        return carry

    lax.fori_loop(0, al, finish, 0)

    for step in range(1, n):
        own_copy(step).wait_send()
    va_copy(0).wait_send()
    va_copy(1).wait_send()

    def drain(j, carry):
        core_copy(j).wait_send()
        return carry

    lax.fori_loop(0, n, drain, 0)


def per_device(slc, disp, times, velocity, amplitude, pair_ends):
    al, _, rows, cols = slc.shape
    n = lax.axis_size("acq")
    lanes = -(-(al * n) // LANES) * LANES
    ext, mid = rows + HALO, rows + LOOK
    zcount = n // GROUP
    vmem = pl.BlockSpec(memory_space=pltpu.VMEM)
    dma = pltpu.SemaphoreType.DMA
    scratch = [
        pltpu.VMEM((n, 3 * al * rows, cols), BF16),
        pltpu.VMEM((n, 3 * al * rows, cols), BF16),
        pltpu.VMEM((n, 8, lanes), F32),
        pltpu.VMEM((n, 8, lanes), F32),
        pltpu.VMEM((2, rows, cols), F32),
        pltpu.VMEM((cols // LANES, 8 * 3 * rows, LANES), F32),
        pltpu.VMEM((cols // LANES, 8 * 3 * rows, LANES), F32),
        pltpu.VMEM((8 * ext, cols), F32),
        pltpu.VMEM((8 * ext, cols), F32),
        pltpu.VMEM((8 * mid, cols), F32),
        pltpu.VMEM((8 * mid, cols), F32),
        pltpu.VMEM((8 * mid, cols), F32),
        pltpu.VMEM((8 * mid, cols), F32),
        pltpu.VMEM((al, 2, 8 * ext, cols), F32),
        pltpu.VMEM((al, 2, 8 * mid, cols), F32),
        pltpu.VMEM((2 * cols, cols), BF16),
        pltpu.VMEM((al * 2 * 8 * mid, 2 * cols), BF16),
        pltpu.VMEM((al * 2 * 8 * mid, cols), F32),
        pltpu.VMEM((al * 2 * 8 * rows, 2 * cols), BF16),
        pltpu.VMEM((al * 2 * 8 * rows, cols), F32),
        pltpu.VMEM((al, 2, 8 * rows, cols), F32),
        pltpu.VMEM((al, 8 * rows, cols), F32),
        pltpu.VMEM((8, lanes), F32),
        dma((n,)), dma((n,)), dma((2,)), dma((2,)),
        dma((n,)), dma((n,)), dma((n,)), dma((n,)),
        pltpu.VMEM((rows, cols), F32),
        pltpu.VMEM((rows, cols), F32),
        pltpu.VMEM(pair_ends.shape[::-1], jnp.int32),
        pltpu.VMEM((8, lanes), F32),
        dma((5,)),
    ]
    hbm = pl.BlockSpec(memory_space=pltpu.HBM)
    grads = pl.pallas_call(
        functools.partial(kernel, n, al, rows, cols, lanes),
        out_shape=(
            jax.ShapeDtypeStruct((al, 2, rows, cols), F32),
            jax.ShapeDtypeStruct((al, rows, cols), F32),
        ),
        in_specs=[hbm, hbm, vmem, hbm, hbm, hbm],
        out_specs=(vmem, vmem),
        scratch_shapes=scratch,
        compiler_params=pltpu.CompilerParams(
            collective_id=0, has_side_effects=True, vmem_limit_bytes=63 * 1024 * 1024
        ),
    )(
        slc.reshape(2 * al * rows, cols),
        disp.reshape(al * rows, cols),
        times.reshape(1, al), velocity, amplitude, pair_ends.T,
    )
    return grads


def solution(mesh):
    return jax.shard_map(
        per_device,
        mesh=mesh,
        in_specs=(
            P("acq", None, ("tiles", "pix"), None),
            P("acq", ("tiles", "pix"), None),
            P("acq"),
            P(("tiles", "pix"), None),
            P(("tiles", "pix"), None),
            P("acq", None),
        ),
        out_specs=(P("acq", None, ("tiles", "pix"), None), P("acq", ("tiles", "pix"), None)),
        check_vma=False,
    )
```

```python
import functools
import math

import jax
import jax.numpy as jnp
from jax import lax
from jax.experimental import pallas as pl
from jax.experimental.pallas import tpu as pltpu
from jax.sharding import PartitionSpec as P

LOOK = 2
GROUP = 2
HALO = 2 * LOOK
LANES = 128
MESH = pl.DeviceIdType.MESH
F32 = jnp.float32
BF16 = jnp.bfloat16
TAU_HI = 6.28125
TAU_LO = 2.0 * math.pi - TAU_HI


def cos_sin(angle):
    turns = jnp.floor(angle * (0.5 / math.pi) + 0.5)
    half = 0.5 * ((angle - turns * TAU_HI) - turns * TAU_LO)
    sq = half * half
    sin_half = jnp.full_like(sq, -1.0 / math.factorial(11))
    for order, sign in ((9, 1.0), (7, -1.0), (5, 1.0), (3, -1.0), (1, 1.0)):
        sin_half = sin_half * sq + sign / math.factorial(order)
    sin_half = sin_half * half
    cos_half = jnp.full_like(sq, 1.0 / math.factorial(12))
    for order, sign in ((10, -1.0), (8, 1.0), (6, -1.0), (4, 1.0), (2, -1.0), (0, 1.0)):
        cos_half = cos_half * sq + sign / math.factorial(order)
    return 1.0 - 2.0 * sin_half * sin_half, 2.0 * sin_half * cos_half


def row_box(values, count):
    pairs = [values[i] + values[i + 1] for i in range(len(values) - 1)]
    out = []
    for i in range(count):
        low = max(0, i - LOOK)
        total, at = None, low
        while at <= i + LOOK:
            if at < i + LOOK:
                piece, at = pairs[at], at + 2
            else:
                piece, at = values[at], at + 1
            total = piece if total is None else total + piece
        out.append(total)
    return out


def put_split(ref, base, values, cols):
    for i in range(0, len(values), 2):
        both = jnp.concatenate([values[i], values[i + 1]], axis=0)
        high = both.astype(BF16)
        low = (both - high.astype(F32)).astype(BF16)
        at = pl.ds(pl.multiple_of(base + 8 * i, 16), 16)
        ref[at, 0:cols] = high
        ref[at, cols : 2 * cols] = low


def kernel(
    n, al, rows, cols, lanes,
    slc_in, disp_in, times_ref, vel_in, amp_in, ends_in,
    grad_ref, dgrad_ref,
    rx, oth, msg, msgr, vah, stg, stg_o, zre, zim, ure, uim, velb, ampb,
    zab, aub, band, lhs, filt, lhs2, filt2, acc, qacc, weights,
    msg_send, msg_recv, va_send, va_recv,
    own_send, blk_recv, of_send, oth_recv,
    vel_ref, amp_ref, ends_ref, t_tile, in_sem,
):
    me = lax.axis_index("acq")
    pix = lax.axis_index("pix")
    zcount = n // GROUP
    mz = me // GROUP
    mx = me % GROUP
    blk_rows = 3 * al * rows
    slc_rows = 2 * al * rows
    wide = 3 * rows
    ext = rows + HALO
    mid = rows + LOOK
    halves = cols // LANES
    core = {"pix": 1 - pix}

    def peer(step):
        return (me + step) % n

    def zchunk(k):
        return mz ^ k

    loads = [
        pltpu.make_async_copy(src, dst, in_sem.at[i])
        for i, (src, dst) in enumerate((
            (ends_in, ends_ref),
            (slc_in, rx.at[me, 0:slc_rows, :]),
            (disp_in, rx.at[me, slc_rows:blk_rows, :]),
            (vel_in, vel_ref),
            (amp_in, amp_ref),
        ))
    ]
    for load in loads:
        load.start()

    barrier = pltpu.get_barrier_semaphore()
    for step in range(1, n):
        pl.semaphore_signal(barrier, inc=1, device_id={"acq": peer(step)}, device_id_type=MESH)
    pl.semaphore_signal(barrier, inc=1, device_id=core, device_id_type=MESH)

    loads[0].wait()
    count = ends_ref.shape[1]
    first = ends_ref[0:1, :]
    second = ends_ref[1:2, :]
    lane = lax.broadcasted_iota(jnp.int32, (lanes, count), 0)
    slot = lax.broadcasted_iota(jnp.int32, (8 * n, count), 0)

    def spread(ids):
        return (ids // al) * 8 + ids % al

    def hot(where):
        return where.astype(F32).astype(BF16)

    contract = (((1,), (1,)), ((), ()))
    counts = lax.dot_general(
        hot(slot == spread(first)), hot(lane == second), contract, preferred_element_type=F32
    ) + lax.dot_general(
        hot(slot == spread(second)), hot(lane == first), contract, preferred_element_type=F32
    )
    t_tile[...] = jnp.zeros_like(t_tile)
    t_tile[al : al + 1, 0:al] = times_ref[...].astype(F32)
    for j in range(n):
        msg[j] = counts[8 * j : 8 * j + 8, :] + t_tile[...]
    msgr[me] = msg[me]

    for load in loads[1:]:
        load.wait()
    pl.semaphore_wait(barrier, n)

    def block_copy(src, dst, send_sem, recv_sem, device):
        return pltpu.make_async_remote_copy(
            src_ref=src, dst_ref=dst, send_sem=send_sem, recv_sem=recv_sem,
            device_id=device, device_id_type=MESH,
        )

    def own_copy(step):
        to = zchunk(step // GROUP) * GROUP + (mx + step) % GROUP
        return block_copy(rx.at[me], rx.at[me], own_send.at[step], blk_recv.at[me], {"acq": to})

    def core_copy(j):
        return block_copy(rx.at[j], oth.at[j], of_send.at[j], oth_recv.at[j], core)

    def msg_copy(step):
        to = peer(step)
        return block_copy(msg.at[to], msgr.at[me], msg_send.at[step], msg_recv.at[me], {"acq": to})

    def va_copy(which):
        src = vel_ref if which == 0 else amp_ref
        return block_copy(src, vah.at[which], va_send.at[which], va_recv.at[which], core)

    va_copy(0).start()
    va_copy(1).start()
    own_copy(1).start()
    core_copy(me).start()
    for step in range(1, n):
        msg_copy(step).start()
    for step in range(2, n):
        own_copy(step).start()

    at_row = lax.broadcasted_iota(jnp.int32, (2 * cols, cols), 0) % cols
    at_col = lax.broadcasted_iota(jnp.int32, (2 * cols, cols), 1)
    band[...] = hot(jnp.abs(at_row - at_col) <= LOOK)
    acc[...] = jnp.zeros_like(acc)
    qacc[...] = jnp.zeros_like(qacc)

    def own_row(i):
        return i + pix * (rows - 1 - 2 * i)

    def nbr_row(i):
        place = 2 * rows - 1 - i
        return place + (1 - pix) * (rows - 1 - 2 * place)

    va_copy(0).wait_recv()
    va_copy(1).wait_recv()
    for i in range(mid):
        for which, src, dst in ((0, vel_ref, velb), (1, amp_ref, ampb)):
            if i < rows:
                line = src[pl.ds(own_row(i), 1), :]
            else:
                line = vah[which, pl.ds(nbr_row(i), 1), :]
            dst[8 * i : 8 * i + 8, :] = jnp.broadcast_to(line, (8, cols))

    for step in range(1, n):
        msg_copy(step).wait_send()
        frm = peer(step)
        block_copy(msg.at[frm], msgr.at[frm], msg_send.at[step], msg_recv.at[frm], {"acq": frm}).wait_recv()
    weights[...] = functools.reduce(lambda a, b: a + b, [msgr[j] for j in range(n)])

    def forward(k, s):
        j = zchunk(k) * GROUP + (mx + s) % GROUP
        block_copy(rx.at[j], rx.at[j], own_send.at[0], blk_recv.at[j], {"acq": j}).wait_recv()
        core_copy(j).start()

    def column_of(row, c):
        l8 = lax.broadcasted_iota(jnp.int32, (8, lanes), 1)
        s8 = lax.broadcasted_iota(jnp.int32, (8, lanes), 0)
        line = jnp.broadcast_to(weights[pl.ds(row, 1), :], (8, lanes))
        return jnp.sum(jnp.where(l8 == c * 8 + s8, line, 0.0), axis=1, keepdims=True)

    def unpack(c):
        for src, dst in ((rx, stg), (oth, stg_o)):
            for s in range(GROUP):
                block = src[c * GROUP + s].astype(F32)
                for h in range(halves):
                    part = block[:, h * LANES : (h + 1) * LANES]
                    for a in range(al):
                        base = (s * al + a) * wide
                        dst[h, base : base + 2 * rows, :] = part[a * 2 * rows : (a + 1) * 2 * rows]
                        dst[h, base + 2 * rows : base + wide, :] = part[
                            slc_rows + a * rows : slc_rows + (a + 1) * rows
                        ]

        def take(i, channel):
            src, row = (stg, own_row(i)) if i < rows else (stg_o, nbr_row(i))
            return jnp.concatenate(
                [src[h, pl.ds(channel * rows + row, 8, stride=wide), :] for h in range(halves)], axis=1
            )

        t_lane = lax.broadcasted_iota(jnp.int32, (8, lanes), 1)
        t_sub = lax.broadcasted_iota(jnp.int32, (8, lanes), 0)
        t_line = jnp.where(
            t_sub < al,
            jnp.broadcast_to(msgr[c * GROUP, al : al + 1, :], (8, lanes)),
            jnp.broadcast_to(msgr[c * GROUP + 1, al : al + 1, :], (8, lanes)),
        )
        when = jnp.sum(jnp.where(t_lane == t_sub % al, t_line, 0.0), axis=1, keepdims=True)
        for i in range(ext):
            zre[8 * i : 8 * i + 8, :] = take(i, 0)
            zim[8 * i : 8 * i + 8, :] = take(i, 1)
            if i < mid:
                u_re, u_im = cos_sin(when * velb[8 * i : 8 * i + 8, :] + take(i, 2))
                ure[8 * i : 8 * i + 8, :] = u_re
                uim[8 * i : 8 * i + 8, :] = u_im

    mean = 1.0 / float((2 * LOOK + 1) ** 2)

    def own_ends():
        def one(a, carry):
            for i in range(ext):
                at = pl.ds(8 * i + al * mx + a, 1)
                for ch, src in ((0, zre), (1, zim)):
                    zab[a, ch, 8 * i : 8 * i + 8, :] = jnp.broadcast_to(src[at, :] * mean, (8, cols))
                if i < mid:
                    for ch, src in ((0, ure), (1, uim)):
                        aub[a, ch, 8 * i : 8 * i + 8, :] = (
                            jnp.broadcast_to(src[at, :], (8, cols)) * ampb[8 * i : 8 * i + 8, :]
                        )
            return carry

        lax.fori_loop(0, al, one, 0)

    def columns(src, span):
        return jnp.dot(src[span, :], band[...], preferred_element_type=F32)

    def tile(i):
        return slice(8 * i, 8 * i + 8)

    def chunk(k, carry):
        c = zchunk(k)

        @pl.when(k + 1 < zcount)
        def _():
            forward(k + 1, 0)
            forward(k + 1, 1)

        for s in range(GROUP):
            core_copy(c * GROUP + s).wait_recv()
        unpack(c)

        @pl.when(k == 0)
        def _():
            own_ends()

        def one(a, carry):
            weight = jnp.broadcast_to(column_of(a, c), (8, cols))
            base = a * (2 * 8 * mid)
            re, im = [], []
            for i in range(ext):
                a_re, a_im = zab[a, 0, tile(i), :], zab[a, 1, tile(i), :]
                b_re, b_im = zre[tile(i), :], zim[tile(i), :]
                re.append(a_re * b_re + a_im * b_im)
                im.append(a_im * b_re - a_re * b_im)
            put_split(lhs, base, row_box(re, mid), cols)
            put_split(lhs, base + 8 * mid, row_box(im, mid), cols)
            span = pl.ds(pl.multiple_of(base, 16), 2 * 8 * mid)
            filt[span, :] = columns(lhs, span)

            re, im = [], []
            for i in range(mid):
                a_re, a_im = aub[a, 0, tile(i), :], aub[a, 1, tile(i), :]
                b_re, b_im = ure[tile(i), :], uim[tile(i), :]
                model_re = b_re * a_re + b_im * a_im
                model_im = b_im * a_re - b_re * a_im
                r_re = filt[pl.ds(pl.multiple_of(base + 8 * i, 8), 8), :] - model_re
                r_im = filt[pl.ds(pl.multiple_of(base + 8 * (mid + i), 8), 8), :] - model_im
                if i < rows:
                    qacc[a, tile(i), :] += weight * (r_re * model_im - r_im * model_re)
                re.append(r_re)
                im.append(r_im)
            base = a * (2 * 8 * rows)
            put_split(lhs2, base, row_box(re, rows), cols)
            put_split(lhs2, base + 8 * rows, row_box(im, rows), cols)
            span = pl.ds(pl.multiple_of(base, 16), 2 * 8 * rows)
            filt2[span, :] = columns(lhs2, span)

            weight = weight * mean
            for i in range(rows):
                g_re = filt2[pl.ds(pl.multiple_of(base + 8 * i, 8), 8), :]
                g_im = filt2[pl.ds(pl.multiple_of(base + 8 * (rows + i), 8), 8), :]
                b_re, b_im = zre[tile(i), :], zim[tile(i), :]
                acc[a, 0, tile(i), :] += weight * (g_re * b_re - g_im * b_im)
                acc[a, 1, tile(i), :] += weight * (g_re * b_im + g_im * b_re)
            return carry

        lax.fori_loop(0, al, one, 0, unroll=True)
        return carry

    forward(0, 1)
    lax.fori_loop(0, zcount, chunk, 0)

    def finish(a, carry):
        for i in range(rows):
            row = pl.ds(own_row(i), 1)
            for ch in range(2):
                grad_ref[a, ch, row, :] = jnp.sum(acc[a, ch, tile(i), :], axis=0, keepdims=True)
            dgrad_ref[a, row, :] = -jnp.sum(qacc[a, tile(i), :], axis=0, keepdims=True)
        return carry

    lax.fori_loop(0, al, finish, 0)

    for step in range(1, n):
        own_copy(step).wait_send()
    va_copy(0).wait_send()
    va_copy(1).wait_send()

    def drain(j, carry):
        core_copy(j).wait_send()
        return carry

    lax.fori_loop(0, n, drain, 0)


def per_device(slc, disp, times, velocity, amplitude, pair_ends):
    al, _, rows, cols = slc.shape
    n = lax.axis_size("acq")
    lanes = -(-(al * n) // LANES) * LANES
    ext, mid = rows + HALO, rows + LOOK
    zcount = n // GROUP
    vmem = pl.BlockSpec(memory_space=pltpu.VMEM)
    dma = pltpu.SemaphoreType.DMA
    scratch = [
        pltpu.VMEM((n, 3 * al * rows, cols), BF16),
        pltpu.VMEM((n, 3 * al * rows, cols), BF16),
        pltpu.VMEM((n, 8, lanes), F32),
        pltpu.VMEM((n, 8, lanes), F32),
        pltpu.VMEM((2, rows, cols), F32),
        pltpu.VMEM((cols // LANES, 8 * 3 * rows, LANES), F32),
        pltpu.VMEM((cols // LANES, 8 * 3 * rows, LANES), F32),
        pltpu.VMEM((8 * ext, cols), F32),
        pltpu.VMEM((8 * ext, cols), F32),
        pltpu.VMEM((8 * mid, cols), F32),
        pltpu.VMEM((8 * mid, cols), F32),
        pltpu.VMEM((8 * mid, cols), F32),
        pltpu.VMEM((8 * mid, cols), F32),
        pltpu.VMEM((al, 2, 8 * ext, cols), F32),
        pltpu.VMEM((al, 2, 8 * mid, cols), F32),
        pltpu.VMEM((2 * cols, cols), BF16),
        pltpu.VMEM((al * 2 * 8 * mid, 2 * cols), BF16),
        pltpu.VMEM((al * 2 * 8 * mid, cols), F32),
        pltpu.VMEM((al * 2 * 8 * rows, 2 * cols), BF16),
        pltpu.VMEM((al * 2 * 8 * rows, cols), F32),
        pltpu.VMEM((al, 2, 8 * rows, cols), F32),
        pltpu.VMEM((al, 8 * rows, cols), F32),
        pltpu.VMEM((8, lanes), F32),
        dma((n,)), dma((n,)), dma((2,)), dma((2,)),
        dma((n,)), dma((n,)), dma((n,)), dma((n,)),
        pltpu.VMEM((rows, cols), F32),
        pltpu.VMEM((rows, cols), F32),
        pltpu.VMEM(pair_ends.shape[::-1], jnp.int32),
        pltpu.VMEM((8, lanes), F32),
        dma((5,)),
    ]
    hbm = pl.BlockSpec(memory_space=pltpu.HBM)
    grads = pl.pallas_call(
        functools.partial(kernel, n, al, rows, cols, lanes),
        out_shape=(
            jax.ShapeDtypeStruct((al, 2, rows, cols), F32),
            jax.ShapeDtypeStruct((al, rows, cols), F32),
        ),
        in_specs=[hbm, hbm, vmem, hbm, hbm, hbm],
        out_specs=(vmem, vmem),
        scratch_shapes=scratch,
        compiler_params=pltpu.CompilerParams(
            collective_id=0, has_side_effects=True, vmem_limit_bytes=63 * 1024 * 1024
        ),
    )(
        slc.reshape(2 * al * rows, cols),
        disp.reshape(al * rows, cols),
        times.reshape(1, al), velocity, amplitude, pair_ends.T,
    )
    return grads


def solution(mesh):
    return jax.shard_map(
        per_device,
        mesh=mesh,
        in_specs=(
            P("acq", None, ("tiles", "pix"), None),
            P("acq", ("tiles", "pix"), None),
            P("acq"),
            P(("tiles", "pix"), None),
            P(("tiles", "pix"), None),
            P("acq", None),
        ),
        out_specs=(P("acq", None, ("tiles", "pix"), None), P("acq", ("tiles", "pix"), None)),
        check_vma=False,
    )
```
